768 devices in a mesh: grid: 24 (over y_hi, z), rep: 32 (over x, y_lo, core).
Axes of the slice: x: 4, y: 8 (y_hi: 2, y_lo: 4; y = y_hi * 4 + y_lo), z: 12, core: 2. Of those that a mesh axis runs over, the one named last changes fastest.
Arguments:
- amplitudes: bfloat16 [96, 960, 960], P('grid', 'rep'), may hold values from -6 to 6
- vvvv_panel: bfloat16 [960, 960, 1920], P('rep', 'grid'), may hold values from -0.01171875 to 0.01171875
- fock_window: bfloat16 [960, 2], P('rep'), may hold values from -0.375 to 0.375
- orbital_irrep: int32 [960], replicated, may hold values from 0 to 3, as said below
- pair_irrep: int32 [96], replicated, may hold values from 0 to 3
- virtual_panel: int32 [2], replicated, may hold values from 0 to 959
Outputs:
- residual: float32 [96, 2, 960], P('rep', None, 'grid')
The draws below stay inside these ranges and needn't reach their ends.
Inputs may be any that keep to these rules, and one draw needn't show every extreme that they name: `orbital_irrep`: the virtual orbitals form four contiguous runs of 240 orbitals each; every orbital of a run has the same irrep, and each irrep 0 to 3 holds exactly one run, in an order that varies from draw to draw.
All inputs are finite; a program needn't handle non-finite values.
Results may differ from the reference program's by a relative error of at most 0.00035.
Values may be sent and summed in bfloat16 or wider, within the bound.
No kernel may reach another device: no remote copies, remote signals or barrier semaphores. Data moves between devices by JAX's collectives and lax.ppermute only.
A program may use at most 64 MiB of HBM per device.

```python
import jax
import jax.numpy as jnp
from jax import lax

V = 960
PAIRS = 96
B_WIN = 2


def draw_orbital_irrep(key, part):
    key = jax.random.fold_in(key, 11)
    order = jax.random.permutation(key, 4).astype(jnp.int32)
    return jnp.repeat(order, V // 4, total_repeat_length=V).astype(jnp.int32)


def set_ends(result, rng, low, high):
    spot = [jax.random.randint(jax.random.fold_in(rng, axis), (), 0, length) for axis, length in enumerate(result.shape)]
    main_axis = result.shape.index(max(result.shape))
    beside = spot[:main_axis] + [(spot[main_axis] + 1) % result.shape[main_axis]] + spot[main_axis + 1:]
    return result.at[tuple(spot)].set(low).at[tuple(beside)].set(high)


def level_of(stream_key, extent, cuts, least, largest):
    def one(dim, shards_of):
        draws = jax.random.uniform(jax.random.fold_in(jax.random.fold_in(stream_key, 6), dim), (shards_of,), jnp.float32, least / len(cuts), largest / len(cuts))
        return jnp.repeat(jnp.exp(draws), extent[dim] // shards_of).reshape((-1,) + (1,) * (len(extent) - dim - 1))

    loudness = one(*cuts[0])
    for cut in cuts[1:]:
        loudness = loudness * one(*cut)
    return loudness


def centred(stream_key, shape, spread, bound, split=(), held_as=jnp.bfloat16):
    loudness = level_of(stream_key, shape, split, -0.22, 0.18) if split else 1.0
    result = jax.random.normal(stream_key, shape, jnp.float32) * spread * loudness
    return jnp.minimum(jnp.maximum(result, -bound), bound).astype(held_as)


def setup_inputs(seed: int = 0) -> dict:
    splits = jax.random.split(jax.random.key(seed), 7)
    return {
        "amplitudes": centred(splits[0], (PAIRS, V, V), 1.0, 6.0, ((0, 24), (1, 32))),
        "vvvv_panel": centred(splits[1], (V, V, B_WIN * V), (V * V // 4) ** -0.5, 0.01171875, ((0, 32), (1, 24))),
        "fock_window": centred(splits[2], (V, B_WIN), (V // 4) ** -0.5, 0.375, ((0, 32),)),
        "orbital_irrep": draw_orbital_irrep(jax.random.fold_in(splits[6], 71), 0),
        "pair_irrep": set_ends(jax.random.randint(splits[4], (PAIRS,), 0, 4), jax.random.fold_in(splits[4], 1), 0, 3).astype(jnp.int32),
        "virtual_panel": jax.random.randint(splits[5], (B_WIN,), 0, V).astype(jnp.int32),
    }


def reference(amplitudes, vvvv_panel, fock_window, orbital_irrep, pair_irrep, virtual_panel):
    panel_irrep = orbital_irrep[virtual_panel]
    pair_sym = jnp.bitwise_xor(orbital_irrep[:, None], orbital_irrep[None, :])
    amp_mask = pair_sym[None, :, :] == pair_irrep[:, None, None]
    masked_amps = jnp.where(amp_mask, amplitudes, jnp.zeros_like(amplitudes))
    target_sym = jnp.bitwise_xor(panel_irrep[:, None], orbital_irrep[None, :])
    target_cols = jnp.transpose(target_sym)
    fock_mask = orbital_irrep[:, None] == panel_irrep[None, :]
    masked_f = jnp.where(fock_mask, fock_window, jnp.zeros_like(fock_window))

    def ladder_step(total, virt_index):
        w_slice = lax.dynamic_index_in_dim(vvvv_panel, virt_index, 0, keepdims=False)
        w_slice = w_slice.reshape(V, B_WIN, V)
        sym_row = lax.dynamic_index_in_dim(pair_sym, virt_index, 0, keepdims=False)
        w_mask = sym_row[None, None, :] == target_cols[:, :, None]
        w_masked = jnp.where(w_mask, w_slice, jnp.zeros_like(w_slice))
        amp_slice = lax.dynamic_index_in_dim(masked_amps, virt_index, 1, keepdims=False)
        term = jnp.einsum("pd,abd->pba", amp_slice.astype(jnp.float32), w_masked.astype(jnp.float32))
        return total + term, None

    start_total = jnp.zeros((PAIRS, B_WIN, V), jnp.float32)
    ladder, _ = lax.scan(ladder_step, start_total, jnp.arange(V, dtype=jnp.int32))
    fock_term = jnp.einsum("pca,cb->pba", masked_amps.astype(jnp.float32), masked_f.astype(jnp.float32))
    return ladder + fock_term
```

```python
import jax
import jax.numpy as jnp
from jax import lax
from jax.sharding import PartitionSpec as P

RUNS = 4
PLANES = 2


def shards(amplitudes, vvvv_panel, fock_window, orbital_irrep, pair_irrep, virtual_panel):
    pair_local, virt_local, full_virt = amplitudes.shape
    col_local = vvvv_panel.shape[1]
    panel_width = vvvv_panel.shape[2] // full_virt
    run = full_virt // RUNS
    groups = lax.axis_size("grid")
    ring = groups // PLANES
    reps = lax.axis_size("rep")
    grid_index = lax.axis_index("grid")
    rep_index = lax.axis_index("rep")

    run_irrep = orbital_irrep[::run]
    row_irrep = orbital_irrep[rep_index * virt_local]
    col_irrep = orbital_irrep[grid_index * col_local]
    panel_irrep = orbital_irrep[virtual_panel]

    own_pairs = lax.dynamic_slice_in_dim(pair_irrep, grid_index * pair_local, pair_local, 0)
    own_want = jnp.bitwise_xor(own_pairs, row_irrep)
    packed = jnp.zeros((pair_local, virt_local, run), amplitudes.dtype)
    for k in range(RUNS):
        packed = jnp.where(
            (own_want == run_irrep[k])[:, None, None], amplitudes[:, :, k * run : (k + 1) * run], packed
        )

    z_groups = [list(range(h * ring, (h + 1) * ring)) for h in range(PLANES)]
    other = lax.ppermute(packed, "grid", [(g, (g + ring) % groups) for g in range(groups)])
    own_ring = lax.all_to_all(
        jnp.broadcast_to(packed[None], (ring, pair_local, virt_local, run)),
        "grid", 0, 0, tiled=True, axis_index_groups=z_groups,
    ).reshape(ring * pair_local, virt_local, run)
    other_ring = lax.all_gather(other, "grid", axis=0, tiled=True, axis_index_groups=z_groups)

    plane = grid_index // ring
    first = jnp.where(plane == 0, own_ring, other_ring)
    second = jnp.where(plane == 0, other_ring, own_ring)
    rows = jnp.concatenate([first, second], axis=0)

    w_want = jnp.bitwise_xor(jnp.bitwise_xor(row_irrep, col_irrep), panel_irrep)
    ladder = []
    for b in range(panel_width):
        start = jnp.argmax(run_irrep == w_want[b]).astype(jnp.int32) * run + b * full_virt
        w_run = lax.dynamic_slice_in_dim(vvvv_panel, start, run, 2)
        keep = pair_irrep == jnp.bitwise_xor(col_irrep, panel_irrep[b])
        part = jnp.einsum("ncd,cad->na", rows, w_run, preferred_element_type=jnp.float32)
        ladder.append(jnp.where(keep[:, None], part, 0.0))
    ladder = jnp.stack(ladder, axis=1)

    own_cols = lax.dynamic_slice_in_dim(rows, (grid_index * col_local) % run, col_local, 2)
    f_keep = row_irrep == panel_irrep
    masked_f = jnp.where(f_keep[None, :], fock_window, jnp.zeros_like(fock_window))
    fock = jnp.einsum("pca,cb->pba", own_cols, masked_f, preferred_element_type=jnp.float32)
    fock = jnp.where((jnp.bitwise_xor(pair_irrep, row_irrep) == col_irrep)[:, None, None], fock, 0.0)
    partial = ladder + fock

    pairs = partial.shape[0]
    out_rows = pairs // reps
    sent = partial.reshape(reps, out_rows * panel_width * col_local)
    got = lax.all_to_all(sent, "rep", 0, 0, tiled=True)
    return jnp.sum(got, axis=0).reshape(out_rows, panel_width, col_local)


def solution(mesh):
    return jax.shard_map(
        shards,
        mesh=mesh,
        in_specs=(P("grid", "rep", None), P("rep", "grid", None), P("rep", None), P(), P(), P()),
        out_specs=P("rep", None, "grid"),
        check_vma=False,
    )
```

```python
import functools

import jax
import jax.numpy as jnp
from jax import lax
from jax.experimental import pallas as pl
from jax.experimental.pallas import tpu as pltpu
from jax.sharding import PartitionSpec as P

RUNS = 4
SIDES = 2
LANES = 128


def pack_kernel(run, orbital_ref, pair_ref, amps_ref, out_ref, held, sem):
    virt_local, pair_local, _ = amps_ref.shape
    row_irrep = orbital_ref[lax.axis_index("rep") * virt_local]
    first_pair = lax.axis_index("grid") * pair_local
    pair_row = lax.broadcasted_iota(jnp.int32, (1, pair_local, run), 1)
    want = jnp.zeros((1, pair_local, run), jnp.int32)
    for p in range(pair_local):
        want = jnp.where(pair_row == p, pair_ref[first_pair + p] ^ row_irrep, want)
    rows = amps_ref[...].astype(jnp.float32)
    best = rows[:, :, :run]
    for k in range(1, RUNS):
        best = jnp.where(want == orbital_ref[k * run], rows[:, :, k * run : (k + 1) * run], best)
    held[...] = best.astype(held.dtype).reshape(held.shape)
    copies = [pltpu.make_async_copy(held, out_ref.at[i], sem.at[i]) for i in range(out_ref.shape[0])]
    for copy in copies:
        copy.start()
    for copy in copies:
        copy.wait()


def panel_kernel(run, width, own, orbital_ref, panel_ref, w_ref, out_ref, held, sem):
    half, cols, span = held.shape[1:]
    grid_index, rep_index = lax.axis_index("grid"), lax.axis_index("rep")
    side = lax.rem(grid_index, SIDES)
    first = (side if own else 1 - side) * half
    row_irrep = orbital_ref[rep_index * (half * SIDES)]
    col_irrep = orbital_ref[grid_index * cols]
    full = run * RUNS
    copies, shifts = [], []
    for b in range(width):
        want = row_irrep ^ col_irrep ^ orbital_ref[panel_ref[b]]
        start = jnp.int32(0)
        for k in range(1, RUNS):
            start = jnp.where(orbital_ref[k * run] == want, k * run, start)
        start = start + b * full
        tile = jnp.minimum(start // LANES, (width * full - span) // LANES)
        lane = pl.multiple_of(tile * LANES, LANES)
        shifts.append(start - lane)
        copies.append(
            pltpu.make_async_copy(w_ref.at[pl.ds(first, half), :, pl.ds(lane, span)], held.at[b], sem.at[b])
        )
        copies[b].start()
    at = lax.broadcasted_iota(jnp.int32, (span, run), 0) - lax.broadcasted_iota(jnp.int32, (span, run), 1)
    for b in range(width):
        pick = jnp.where(at == shifts[b], 1.0, 0.0).astype(jnp.bfloat16)
        copies[b].wait()
        block = held[b].astype(jnp.float32).reshape(half * cols, span).astype(jnp.bfloat16)
        moved = jnp.dot(block, pick, preferred_element_type=jnp.float32)
        out_ref[:, b * cols : (b + 1) * cols, :] = moved.reshape(half, cols, run).astype(out_ref.dtype)


def shards(amplitudes, vvvv_panel, fock_window, orbital_irrep, pair_irrep, virtual_panel):
    pair_local, virt_local, full_virt = amplitudes.shape
    col_local = vvvv_panel.shape[1]
    panel_width = vvvv_panel.shape[2] // full_virt
    run = full_virt // RUNS
    groups = lax.axis_size("grid")
    reps = lax.axis_size("rep")
    half = virt_local // SIDES
    span = LANES * (-(-(run + LANES - 1) // LANES))
    dtype = amplitudes.dtype
    grid_index = lax.axis_index("grid")
    rep_index = lax.axis_index("rep")
    side = grid_index % SIDES

    smem = pl.BlockSpec(memory_space=pltpu.SMEM)
    vmem = pl.BlockSpec(memory_space=pltpu.VMEM)
    anywhere = pl.BlockSpec(memory_space=pl.ANY)
    copies = groups // SIDES
    sent = pl.pallas_call(
        functools.partial(pack_kernel, run),
        out_shape=jax.ShapeDtypeStruct((copies, SIDES, half, pair_local, run), dtype),
        in_specs=[smem, smem, vmem],
        out_specs=anywhere,
        scratch_shapes=[pltpu.VMEM((SIDES, half, pair_local, run), dtype), pltpu.SemaphoreType.DMA((copies,))],
    )(orbital_irrep, pair_irrep, amplitudes.transpose(1, 0, 2))
    rows = lax.all_to_all(sent.reshape(groups, half, pair_local, run), "grid", 0, 0, tiled=True)

    def window(own):
        return pl.pallas_call(
            functools.partial(panel_kernel, run, panel_width, own),
            out_shape=jax.ShapeDtypeStruct((half, panel_width * col_local, run), dtype),
            in_specs=[smem, smem, anywhere],
            out_specs=vmem,
            scratch_shapes=[
                pltpu.VMEM((panel_width, half, col_local, span), dtype),
                pltpu.SemaphoreType.DMA((panel_width,)),
            ],
            compiler_params=pltpu.CompilerParams(vmem_limit_bytes=32 * 1024 * 1024),
        )(orbital_irrep, virtual_panel, vvvv_panel)

    other = lax.ppermute(window(False), "grid", [(g, g ^ 1) for g in range(groups)])
    kept = window(True)

    row_irrep = orbital_irrep[rep_index * virt_local]
    col_irrep = orbital_irrep[grid_index * col_local]
    panel_irrep = orbital_irrep[virtual_panel]
    own_fock = lax.dynamic_slice_in_dim(fock_window, side * half, half, 0)
    own_fock = jnp.where((row_irrep == panel_irrep)[None, :], own_fock, jnp.zeros_like(own_fock))

    def fock_cols(which):
        col = (which * col_local) % run + jnp.arange(col_local)
        hit = col[None, None, :, None] == jnp.arange(run)
        picked = jnp.where(hit, own_fock[:, :, None, None], jnp.zeros((), dtype))
        return picked.reshape(half, panel_width * col_local, run)

    def product(cols, which):
        left = jnp.einsum("gcjd,cxd->gjx", rows, cols, preferred_element_type=jnp.float32)
        right = jnp.einsum("gcjd,cxd->gjx", rows, fock_cols(which), preferred_element_type=jnp.float32)
        return (left + right).reshape(-1, panel_width * col_local)

    own_part = product(kept, grid_index)
    other_part = product(other, grid_index + 1 - 2 * side)
    partial = jnp.stack([jnp.where(side == 0, own_part, other_part), jnp.where(side == 0, other_part, own_part)])
    keep = pair_irrep[:, None] == jnp.bitwise_xor(col_irrep, panel_irrep)[None, :]
    partial = jnp.where(jnp.repeat(keep, col_local, axis=1)[None], partial, 0.0)

    out_rows = partial.shape[1] // reps
    outgoing = partial.reshape(SIDES * reps, out_rows * panel_width * col_local)
    teams = [
        [(first + s) * reps + r for s in range(SIDES) for r in range(reps)]
        for first in range(0, groups, SIDES)
    ]
    got = lax.all_to_all(outgoing, ("grid", "rep"), 0, 0, tiled=True, axis_index_groups=teams)
    return jnp.sum(got, axis=0).reshape(out_rows, panel_width, col_local)


def solution(mesh):
    return jax.shard_map(
        shards,
        mesh=mesh,
        in_specs=(P("grid", "rep", None), P("rep", "grid", None), P("rep", None), P(), P(), P()),
        out_specs=P("rep", None, "grid"),
        check_vma=False,
    )
```

```python
import functools

import jax
import jax.numpy as jnp
from jax import lax
from jax.experimental import pallas as pl
from jax.experimental.pallas import tpu as pltpu
from jax.sharding import PartitionSpec as P

RUNS = 4
SIDES = 2
LANES = 128


def pack_kernel(run, orbital_ref, pair_ref, amps_ref, out_ref, held, sem):
    virt_local, pair_local, _ = amps_ref.shape
    row_irrep = orbital_ref[lax.axis_index("rep") * virt_local]
    first_pair = lax.axis_index("grid") * pair_local
    pair_row = lax.broadcasted_iota(jnp.int32, (1, pair_local, run), 1)
    want = jnp.zeros((1, pair_local, run), jnp.int32)
    for p in range(pair_local):
        want = jnp.where(pair_row == p, pair_ref[first_pair + p] ^ row_irrep, want)
    rows = amps_ref[...].astype(jnp.float32)
    best = rows[:, :, :run]
    for k in range(1, RUNS):
        best = jnp.where(want == orbital_ref[k * run], rows[:, :, k * run : (k + 1) * run], best)
    held[...] = best.astype(held.dtype).reshape(held.shape)
    copies = [pltpu.make_async_copy(held, out_ref.at[i], sem.at[i]) for i in range(out_ref.shape[0])]
    for copy in copies:
        copy.start()
    for copy in copies:
        copy.wait()


def panel_kernel(run, width, own, orbital_ref, panel_ref, w_ref, out_ref, held, sem):
    half, cols, span = held.shape[1:]
    grid_index, rep_index = lax.axis_index("grid"), lax.axis_index("rep")
    side = lax.rem(grid_index, SIDES)
    first = (side if own else 1 - side) * half
    row_irrep = orbital_ref[rep_index * (half * SIDES)]
    col_irrep = orbital_ref[grid_index * cols]
    full = run * RUNS
    copies, shifts = [], []
    for b in range(width):
        want = row_irrep ^ col_irrep ^ orbital_ref[panel_ref[b]]
        start = jnp.int32(0)
        for k in range(1, RUNS):
            start = jnp.where(orbital_ref[k * run] == want, k * run, start)
        start = start + b * full
        tile = jnp.minimum(start // LANES, (width * full - span) // LANES)
        lane = pl.multiple_of(tile * LANES, LANES)
        shifts.append(start - lane)
        copies.append(
            pltpu.make_async_copy(w_ref.at[pl.ds(first, half), :, pl.ds(lane, span)], held.at[b], sem.at[b])
        )
        copies[b].start()
    at = lax.broadcasted_iota(jnp.int32, (span, run), 0) - lax.broadcasted_iota(jnp.int32, (span, run), 1)
    for b in range(width):
        pick = jnp.where(at == shifts[b], 1.0, 0.0).astype(jnp.bfloat16)
        copies[b].wait()
        block = held[b].astype(jnp.float32).reshape(half * cols, span).astype(jnp.bfloat16)
        moved = jnp.dot(block, pick, preferred_element_type=jnp.float32)
        out_ref[:, b * cols : (b + 1) * cols, :] = moved.reshape(half, cols, run).astype(out_ref.dtype)


def shards(amplitudes, vvvv_panel, fock_window, orbital_irrep, pair_irrep, virtual_panel):
    pair_local, virt_local, full_virt = amplitudes.shape
    col_local = vvvv_panel.shape[1]
    panel_width = vvvv_panel.shape[2] // full_virt
    run = full_virt // RUNS
    groups = lax.axis_size("grid")
    reps = lax.axis_size("rep")
    half = virt_local // SIDES
    span = LANES * (-(-(run + LANES - 1) // LANES))
    dtype = amplitudes.dtype
    grid_index = lax.axis_index("grid")
    rep_index = lax.axis_index("rep")
    side = grid_index % SIDES

    smem = pl.BlockSpec(memory_space=pltpu.SMEM)
    vmem = pl.BlockSpec(memory_space=pltpu.VMEM)
    anywhere = pl.BlockSpec(memory_space=pl.ANY)
    copies = groups // SIDES
    sent = pl.pallas_call(
        functools.partial(pack_kernel, run),
        out_shape=jax.ShapeDtypeStruct((copies, SIDES, half, pair_local, run), dtype),
        in_specs=[smem, smem, vmem],
        out_specs=anywhere,
        scratch_shapes=[pltpu.VMEM((SIDES, half, pair_local, run), dtype), pltpu.SemaphoreType.DMA((copies,))],
    )(orbital_irrep, pair_irrep, amplitudes.transpose(1, 0, 2))
    rows = lax.all_to_all(sent.reshape(groups, half, pair_local, run), "grid", 0, 0, tiled=True)

    def window(own):
        return pl.pallas_call(
            functools.partial(panel_kernel, run, panel_width, own),
            out_shape=jax.ShapeDtypeStruct((half, panel_width * col_local, run), dtype),
            in_specs=[smem, smem, anywhere],
            out_specs=vmem,
            scratch_shapes=[
                pltpu.VMEM((panel_width, half, col_local, span), dtype),
                pltpu.SemaphoreType.DMA((panel_width,)),
            ],
            compiler_params=pltpu.CompilerParams(vmem_limit_bytes=60 * 1024 * 1024),
        )(orbital_irrep, virtual_panel, vvvv_panel)

    swap = [(g, g ^ 1) for g in range(groups)]
    send_w = window(False)
    cut = -(-half // 1)
    other = [lax.ppermute(send_w[i : min(i + cut, half)], "grid", swap) for i in range(0, half, cut)]
    other = jnp.concatenate(other, axis=0)
    kept = window(True)

    row_irrep = orbital_irrep[rep_index * virt_local]
    col_irrep = orbital_irrep[grid_index * col_local]
    panel_irrep = orbital_irrep[virtual_panel]
    own_fock = lax.dynamic_slice_in_dim(fock_window, side * half, half, 0)
    own_fock = jnp.where((row_irrep == panel_irrep)[None, :], own_fock, jnp.zeros_like(own_fock))

    def fock_cols(which):
        col = (which * col_local) % run + jnp.arange(col_local)
        hit = col[None, None, :, None] == jnp.arange(run)
        picked = jnp.where(hit, own_fock[:, :, None, None], jnp.zeros((), dtype))
        return picked.reshape(half, panel_width * col_local, run)

    def product(cols, which):
        left = jnp.einsum("gcjd,cxd->gjx", rows, cols, preferred_element_type=jnp.float32)
        right = jnp.einsum("gcjd,cxd->gjx", rows, fock_cols(which), preferred_element_type=jnp.float32)
        return (left + right).reshape(-1, panel_width * col_local)

    own_part = product(kept, grid_index)
    other_part = product(other, grid_index + 1 - 2 * side)
    partial = jnp.stack([jnp.where(side == 0, own_part, other_part), jnp.where(side == 0, other_part, own_part)])
    keep = pair_irrep[:, None] == jnp.bitwise_xor(col_irrep, panel_irrep)[None, :]
    partial = jnp.where(jnp.repeat(keep, col_local, axis=1)[None], partial, 0.0)

    out_rows = partial.shape[1] // reps
    outgoing = partial.reshape(SIDES * reps, out_rows * panel_width * col_local)
    teams = [
        [(first + s) * reps + r for s in range(SIDES) for r in range(reps)]
        for first in range(0, groups, SIDES)
    ]
    got = lax.all_to_all(outgoing, ("grid", "rep"), 0, 0, tiled=True, axis_index_groups=teams)
    return jnp.sum(got, axis=0).reshape(out_rows, panel_width, col_local)


def solution(mesh):
    return jax.shard_map(
        shards,
        mesh=mesh,
        in_specs=(P("grid", "rep", None), P("rep", "grid", None), P("rep", None), P(), P(), P()),
        out_specs=P("rep", None, "grid"),
        check_vma=False,
    )
```
